512 devices in a mesh: ctx: 32 (over x_lo, z), exp: 16 (over y, x_hi, core).
Axes of the slice: x: 4 (x_hi: 2, x_lo: 2; x = x_hi * 2 + x_lo), y: 4, z: 16, core: 2. Of those that a mesh axis runs over, the one named last changes fastest.
Arguments:
- queries: bfloat16 [32, 2048, 2048], P('exp', 'ctx'), may hold values from -128 to 128
- key_vectors: bfloat16 [32, 2048, 256], P('exp', 'ctx'), may hold values from -8 to 8
- value_vectors: bfloat16 [32, 2048, 256], P('exp', 'ctx'), may hold values from -4 to 4
- output_grad: bfloat16 [32, 2048, 2048], P('exp', 'ctx'), may hold values from -6 to 6
- doc_lengths: int32 [32, 8], P('exp'), may hold values from 1 to 1024, 2048 in all within a row
- expert_input: bfloat16 [65536, 2048], P(('ctx', 'exp')), may hold values from -6 to 6
- expert_grad: bfloat16 [65536, 2048], P(('ctx', 'exp')), may hold values from -6 to 6
- expert_pick: int32 [65536], P(('ctx', 'exp')), may hold values from 0 to 15, as said below
- gate_weight: float32 [65536], P(('ctx', 'exp')), may hold values from 0.1 to 1
- gate_matrix: bfloat16 [16, 2048, 384], P('exp', 'ctx'), may hold values from -0.125 to 0.125
- up_matrix: bfloat16 [16, 2048, 384], P('exp', 'ctx'), may hold values from -0.125 to 0.125
- down_matrix: bfloat16 [16, 384, 2048], P('exp', None, 'ctx'), may hold values from -0.3125 to 0.3125
Outputs:
- query_grad: bfloat16 [32, 2048, 2048], P('exp', 'ctx')
- key_grad: bfloat16 [32, 2048, 256], P('exp', 'ctx')
- value_grad: bfloat16 [32, 2048, 256], P('exp', 'ctx')
- input_grad: bfloat16 [65536, 2048], P(('ctx', 'exp'))
The draws below stay inside these ranges and needn't reach their ends.
Inputs may be any that keep to these rules, and one draw needn't show every extreme that they name: `expert_pick`: one expert of this round lives on each index of exp. Among the rows of one device one expert, the same on every device and drawn from the seed, is picked by exactly 16 rows, and the other experts share the remaining rows evenly, within one row.
All inputs are finite; a program needn't handle non-finite values.
Results may differ from the reference program's by a relative error of at most 0.0057.
Values may be sent and summed in bfloat16 or wider, within the bound.
No kernel may reach another device: no remote copies, remote signals or barrier semaphores. Data moves between devices by JAX's collectives and lax.ppermute only.
A program may use at most 64 MiB of HBM per device.

```python
import math
import jax
import jax.numpy as jnp
import numpy as np
from jax import lax

D = 2048
FF = 384
QUERY_HEADS = 16
KEY_VALUE_HEADS = 2
HEAD_WIDTH = 128
TOK_DEV = 128
NDOC = 8
SEQUENCE_LENGTH = 2048
DOC_MOST = 1024
CAP = 16
SEQUENCE_COUNT = 32
TOKENS = 65536
N_EXP = 16


def shared_keys(key):
    base_offset = jax.random.normal(jax.random.fold_in(key, 101), (SEQUENCE_COUNT, SEQUENCE_LENGTH, KEY_VALUE_HEADS, HEAD_WIDTH), jnp.float32)
    return jnp.clip(base_offset, -4.0, 4.0)


def draw_key_vectors(key, part):
    base_offset = shared_keys(key)
    return base_offset.reshape(SEQUENCE_COUNT, SEQUENCE_LENGTH, KEY_VALUE_HEADS * HEAD_WIDTH).astype(jnp.bfloat16)


def draw_queries(key, part):
    key = jax.random.fold_in(key, 5)
    values = jnp.clip(jax.random.normal(key, (SEQUENCE_COUNT, SEQUENCE_LENGTH, QUERY_HEADS, HEAD_WIDTH), jnp.float32), -4.0, 4.0)
    return values.reshape(SEQUENCE_COUNT, SEQUENCE_LENGTH, QUERY_HEADS * HEAD_WIDTH).astype(jnp.bfloat16)


def draw_expert_pick(key, part):
    key = jax.random.fold_in(key, 3)
    blocks = TOKENS // TOK_DEV
    rounds = 2 * TOK_DEV // CAP
    hottest = jax.random.randint(jax.random.fold_in(key, 1), (), 0, rounds)
    block_keys = jax.random.split(jax.random.fold_in(key, 2), blocks)
    order = jax.vmap(lambda single: jax.random.permutation(single, TOK_DEV))(block_keys)
    offset = jax.random.randint(jax.random.fold_in(key, 4), (blocks, 1), 0, rounds - 1)
    other = (order - CAP + offset) % (rounds - 1)
    other = other + (other >= hottest).astype(jnp.int32)
    picks = jnp.where(order < CAP, hottest, other)
    return picks.reshape(TOKENS).astype(jnp.int32)


def shard_levels(stream_key, shape, cuts, low, largest):
    factor_of, own = 1.0, jax.random.fold_in(stream_key, 6)
    for dim, parts in cuts:
        steps = jnp.exp(jax.random.uniform(jax.random.fold_in(own, dim), (parts,), jnp.float32, low / len(cuts), largest / len(cuts)))
        factor_of = factor_of * jnp.repeat(steps, shape[dim] // parts).reshape([-1 if axis == dim else 1 for axis in range(len(shape))])
    return factor_of


def length_profile(amount, total, most, skew):
    weights = [(1 << 20) // math.isqrt(rank ** skew) + 1 for rank in range(2, amount + 1)]
    rest, counts = total - most - (amount - 1), [1] * (amount - 1)
    while rest > 0:
        free = [i for i in range(amount - 1) if counts[i] < most]
        pool, remaining = sum([weights[i] for i in free]), rest
        for i in free:
            more = min(most - counts[i], max(1, remaining * weights[i] // pool), rest)
            counts[i] = counts[i] + more
            rest = rest - more
    return np.array([most] + counts)


def uneven_parts(rng, count, total, bound, slope):
    if count == 2:
        one = jax.random.randint(rng, (), max(1, total - bound), min(bound, total - 1) + 1)
        return jnp.stack([one, total - one])
    sizes = jnp.asarray(length_profile(count, total, bound, slope), jnp.int32)
    pairs = (count - 1) // 2
    source_of, taker = sizes[1:1 + 2 * pairs:2], sizes[2:2 + 2 * pairs:2]
    margin = jnp.minimum(source_of - 1, bound - taker)
    passed = jax.random.randint(jax.random.fold_in(rng, 1), (pairs,), 0, 1 << 20) % (margin + 1)
    sizes = sizes.at[1:1 + 2 * pairs:2].set(source_of - passed).at[2:2 + 2 * pairs:2].set(taker + passed)
    return sizes[jax.random.permutation(jax.random.fold_in(rng, 2), count)]


def scatter_about(key, extent, width, reach, pieces=(), kind=jnp.bfloat16):
    values = jax.random.normal(key, extent, jnp.float32) * width
    if len(pieces) > 0:
        values = shard_levels(key, extent, pieces, -0.22, 0.18) * values
    return jnp.clip(values, min=-reach, max=reach).astype(kind)


def setup_inputs(seed: int = 0) -> dict:
    keys = jax.random.split(jax.random.key(seed), 13)
    return {
        "queries": draw_queries(jax.random.fold_in(keys[12], 71), 0),
        "key_vectors": draw_key_vectors(jax.random.fold_in(keys[12], 71), 0),
        "value_vectors": scatter_about(keys[2], (SEQUENCE_COUNT, SEQUENCE_LENGTH, KEY_VALUE_HEADS * HEAD_WIDTH), 1.0, 4.0, ((0, 16), (1, 32))),
        "output_grad": scatter_about(keys[3], (SEQUENCE_COUNT, SEQUENCE_LENGTH, QUERY_HEADS * HEAD_WIDTH), 1.0, 6.0, ((0, 16), (1, 32))),
        "doc_lengths": jax.vmap(lambda own: uneven_parts(own, NDOC, SEQUENCE_LENGTH, DOC_MOST, 2))(jax.random.split(keys[4], SEQUENCE_COUNT)).reshape((SEQUENCE_COUNT, NDOC)).astype(jnp.int32),
        "expert_input": scatter_about(keys[5], (TOKENS, D), 1.0, 6.0, ((0, 512),)),
        "expert_grad": scatter_about(keys[6], (TOKENS, D), 1.0, 6.0, ((0, 512),)),
        "expert_pick": draw_expert_pick(jax.random.fold_in(keys[12], 71), 0),
        "gate_weight": jnp.clip(jnp.exp(math.log(1.0) - 2.3025851 * jax.random.uniform(keys[8], (TOKENS,), jnp.float32) ** shard_levels(keys[8], (TOKENS,), ((0, 512),), -0.2, 0.2)), 0.1, 1.0),
        "gate_matrix": scatter_about(keys[9], (N_EXP, D, FF), D ** -0.5, 0.125, ((0, 16), (1, 32))),
        "up_matrix": scatter_about(keys[10], (N_EXP, D, FF), D ** -0.5, 0.125, ((0, 16), (1, 32))),
        "down_matrix": scatter_about(keys[11], (N_EXP, FF, D), FF ** -0.5, 0.3125, ((0, 16), (2, 32))),
    }


def document_ids(lengths):
    starts = jnp.cumsum(lengths) - lengths
    position = jnp.arange(SEQUENCE_LENGTH, dtype=jnp.int32)
    documents = lax.optimization_barrier(jnp.sum((position[:, None] >= starts[None, :]).astype(jnp.int32), axis=1)) - 1
    return documents

def head_grads(query_head, key_head, value_head, grad_head, visible):
    scale = 1.0 / math.sqrt(HEAD_WIDTH)
    scores = jnp.dot(query_head, key_head.T, preferred_element_type=jnp.float32) * scale
    scores = jnp.where(visible, scores, -1e+30)
    highest = lax.optimization_barrier(jnp.max(scores, axis=1, keepdims=True))
    weights = jnp.where(visible, jnp.exp(scores - highest), 0.0)
    probs = weights / lax.optimization_barrier(jnp.sum(weights, axis=1, keepdims=True))
    dprobs = jnp.dot(grad_head, value_head.T, preferred_element_type=jnp.float32)
    delta = lax.optimization_barrier(jnp.sum(probs * dprobs, axis=1, keepdims=True))
    dscores = (probs * (dprobs - delta)).astype(jnp.bfloat16)
    probs_low = probs.astype(jnp.bfloat16)
    value_part = jnp.dot(probs_low.T, grad_head, preferred_element_type=jnp.float32)
    query_part = jnp.dot(dscores, key_head, preferred_element_type=jnp.float32) * scale
    key_part = jnp.dot(dscores.T, query_head, preferred_element_type=jnp.float32) * scale
    return (query_part, key_part, value_part)

def sequence_grads(item):
    queries, key_vectors, value_vectors, output_grad, lengths = item
    documents = document_ids(lengths)
    position = jnp.arange(SEQUENCE_LENGTH, dtype=jnp.int32)
    visible = (position[None, :] <= position[:, None]) & (documents[None, :] == documents[:, None])
    group_share = QUERY_HEADS // KEY_VALUE_HEADS
    query_heads = queries.reshape(SEQUENCE_LENGTH, QUERY_HEADS, HEAD_WIDTH).transpose(1, 0, 2)
    grad_heads = output_grad.reshape(SEQUENCE_LENGTH, QUERY_HEADS, HEAD_WIDTH).transpose(1, 0, 2)
    key_head_rows = key_vectors.reshape(SEQUENCE_LENGTH, KEY_VALUE_HEADS, HEAD_WIDTH).transpose(1, 0, 2)
    value_head_rows = value_vectors.reshape(SEQUENCE_LENGTH, KEY_VALUE_HEADS, HEAD_WIDTH).transpose(1, 0, 2)

    def one_head(index):
        group = index // group_share
        return head_grads(query_heads[index], key_head_rows[group], value_head_rows[group], grad_heads[index], visible)
    query_parts, key_portions, value_portions = lax.map(one_head, jnp.arange(QUERY_HEADS, dtype=jnp.int32))
    key_grand_sum = lax.optimization_barrier(jnp.sum(key_portions.reshape(KEY_VALUE_HEADS, group_share, SEQUENCE_LENGTH, HEAD_WIDTH), axis=1))
    value_grand_sum = lax.optimization_barrier(jnp.sum(value_portions.reshape(KEY_VALUE_HEADS, group_share, SEQUENCE_LENGTH, HEAD_WIDTH), axis=1))
    query_out = query_parts.astype(jnp.bfloat16).transpose(1, 0, 2).reshape(SEQUENCE_LENGTH, QUERY_HEADS * HEAD_WIDTH)
    key_result = key_grand_sum.astype(jnp.bfloat16).transpose(1, 0, 2).reshape(SEQUENCE_LENGTH, KEY_VALUE_HEADS * HEAD_WIDTH)
    value_result = value_grand_sum.astype(jnp.bfloat16).transpose(1, 0, 2).reshape(SEQUENCE_LENGTH, KEY_VALUE_HEADS * HEAD_WIDTH)
    return (query_out, key_result, value_result)

def activation_grads(act_grad, gate_act, up_act):
    sigmoid_gate = jax.nn.sigmoid(gate_act)
    up_grad = (act_grad * gate_act * sigmoid_gate).astype(jnp.bfloat16)
    gate_grad = (act_grad * up_act * sigmoid_gate * (1.0 + gate_act * (1.0 - sigmoid_gate))).astype(jnp.bfloat16)
    return (gate_grad, up_grad)

def reference(queries, key_vectors, value_vectors, output_grad, doc_lengths, expert_input, expert_grad, expert_pick, gate_weight, gate_matrix, up_matrix, down_matrix):
    query_grad, key_grad, value_grad = lax.map(sequence_grads, (queries, key_vectors, value_vectors, output_grad, doc_lengths))
    scaled_grad = (gate_weight[:, None] * expert_grad.astype(jnp.float32)).astype(jnp.bfloat16)
    limit = CAP * (TOKENS // TOK_DEV)

    def one_expert(total, index):
        picked = expert_pick == index
        chosen = jnp.nonzero(picked, size=limit, fill_value=0)[0].astype(jnp.int32)
        filled = jnp.arange(limit, dtype=jnp.int32) < jnp.sum(picked.astype(jnp.int32))
        rows = expert_input[chosen]
        grads = scaled_grad[chosen]
        gate_act = jnp.dot(rows, gate_matrix[index], preferred_element_type=jnp.float32)
        up_act = jnp.dot(rows, up_matrix[index], preferred_element_type=jnp.float32)
        act_grad = jnp.dot(grads, down_matrix[index].T, preferred_element_type=jnp.float32)
        gate_grad, up_grad = activation_grads(act_grad, gate_act, up_act)
        result = jnp.dot(gate_grad, gate_matrix[index].T, preferred_element_type=jnp.float32)
        result = result + jnp.dot(up_grad, up_matrix[index].T, preferred_element_type=jnp.float32)
        result = result.astype(jnp.bfloat16).astype(jnp.float32)
        total = total.at[chosen].add(jnp.where(filled[:, None], result, 0.0))
        return (total, None)
    start_total = jnp.zeros((TOKENS, D), jnp.float32)
    total, unused = lax.scan(one_expert, start_total, jnp.arange(N_EXP, dtype=jnp.int32))
    input_grad = total.astype(jnp.bfloat16)
    return (query_grad, key_grad, value_grad, input_grad)
```

```python
import functools
import math

import jax
import jax.numpy as jnp
from jax import lax
from jax.experimental import pallas as pl
from jax.experimental.pallas import tpu as pltpu
from jax.sharding import PartitionSpec as P

HEADS = 16
KV_HEADS = 2
WIDTH = 128
SHARE = HEADS // KV_HEADS
BLOCK = 128
RING = 8
LANES = SHARE * BLOCK
MOST = 9
SCALE = 1.0 / math.sqrt(WIDTH)

X_PAIRS = [[z, 16 + z] for z in range(16)]
Z_LINES = [[x * 16 + z for z in range(16)] for x in range(2)]
QUADS = [[2 * j, 2 * j + 1, 16 + 2 * j, 16 + 2 * j + 1] for j in range(8)]
RINGS = [[x * 16 + 2 * j + p for j in range(8)] for x in range(2) for p in range(2)]


def z_shift(step):
    return [(x * 16 + z, x * 16 + (z + step) % 16) for x in range(2) for z in range(16)]


NT = (((1,), (1,)), ((), ()))
TN = (((0,), (0,)), ((), ()))


def attention_kernel(
    lengths_ref, place_ref, qg_ref, kv_ref, dq_ref, dkv_ref, q_rows, g_rows, prob, dprob, acc
):
    ring = place_ref[0]
    sequence = place_ref[1]
    starts = [jnp.int32(0)]
    for d in range(7):
        starts.append(starts[-1] + lengths_ref[sequence, d])
    acc[...] = jnp.zeros_like(acc)
    for half in range(2):
        query_block = ring + RING * half
        first = query_block * BLOCK
        rows = pl.ds(half * BLOCK, BLOCK)
        for h in range(SHARE):
            q_rows[h * BLOCK : (h + 1) * BLOCK, :] = qg_ref[rows, h * WIDTH : (h + 1) * WIDTH]
            g_rows[h * BLOCK : (h + 1) * BLOCK, :] = qg_ref[
                rows, (SHARE + h) * WIDTH : (SHARE + h + 1) * WIDTH
            ]
        lane = lax.broadcasted_iota(jnp.int32, (1, LANES), 1)
        position = first + lane % BLOCK
        begin = jnp.zeros((1, LANES), jnp.int32)
        low = jnp.int32(0)
        for start in starts:
            begin = jnp.where(position >= start, start, begin)
            low = jnp.where(first >= start, start, low)
        low_block = low // BLOCK
        count = query_block - low_block + 1

        def tile(i):
            block = low_block + i
            return (ring - block) & (RING - 1), pl.multiple_of((block // RING) * BLOCK, BLOCK), block

        def score_step(i, highest):
            slot, offset, block = tile(i)
            keys = kv_ref[slot, pl.ds(offset, BLOCK), 0:WIDTH]
            values = kv_ref[slot, pl.ds(offset, BLOCK), WIDTH : 2 * WIDTH]
            scores = (
                lax.dot_general(keys, q_rows[...], NT, preferred_element_type=jnp.float32) * SCALE
            )
            at = block * BLOCK + lax.broadcasted_iota(jnp.int32, (BLOCK, LANES), 0)
            scores = jnp.where((at >= begin) & (at <= position), scores, -1e30)
            prob[i] = scores
            dprob[i] = lax.dot_general(
                values, g_rows[...], NT, preferred_element_type=jnp.float32
            )
            return jnp.maximum(highest, jnp.max(scores, axis=0, keepdims=True))

        highest = lax.fori_loop(0, count, score_step, jnp.full((1, LANES), -1e30, jnp.float32))

        def sum_step(i, carry):
            total, weighted = carry
            weights = jnp.exp(prob[i] - highest)
            prob[i] = weights
            return (
                total + jnp.sum(weights, axis=0, keepdims=True),
                weighted + jnp.sum(weights * dprob[i], axis=0, keepdims=True),
            )

        zero = jnp.zeros((1, LANES), jnp.float32)
        total, weighted = lax.fori_loop(0, count, sum_step, (zero, zero))
        inverse = 1.0 / total
        delta = weighted * inverse

        def grad_step(i, query_acc):
            slot, offset, block = tile(i)
            keys = kv_ref[slot, pl.ds(offset, BLOCK), 0:WIDTH]
            probs = prob[i] * inverse
            dscores = (probs * (dprob[i] - delta)).astype(jnp.bfloat16)
            home = block & (RING - 1)
            acc[home, pl.ds(offset, BLOCK), 0:WIDTH] += (
                jnp.dot(dscores, q_rows[...], preferred_element_type=jnp.float32) * SCALE
            )
            acc[home, pl.ds(offset, BLOCK), WIDTH : 2 * WIDTH] += jnp.dot(
                probs.astype(jnp.bfloat16), g_rows[...], preferred_element_type=jnp.float32
            )
            return query_acc + lax.dot_general(
                keys, dscores, TN, preferred_element_type=jnp.float32
            )

        query_acc = lax.fori_loop(0, count, grad_step, jnp.zeros((WIDTH, LANES), jnp.float32))
        query_acc = (query_acc * SCALE).T.astype(jnp.bfloat16)
        for h in range(SHARE):
            dq_ref[rows, h * WIDTH : (h + 1) * WIDTH] = query_acc[h * BLOCK : (h + 1) * BLOCK, :]
    dkv_ref[...] = acc[...].astype(jnp.bfloat16)


def attention(lengths, place, qg, kv):
    vmem = pl.BlockSpec(memory_space=pltpu.VMEM)
    smem = pl.BlockSpec(memory_space=pltpu.SMEM)
    return pl.pallas_call(
        attention_kernel,
        out_shape=(
            jax.ShapeDtypeStruct((2 * BLOCK, SHARE * WIDTH), jnp.bfloat16),
            jax.ShapeDtypeStruct((RING, 2 * BLOCK, 2 * WIDTH), jnp.bfloat16),
        ),
        in_specs=[smem, smem, vmem, vmem],
        out_specs=(vmem, vmem),
        scratch_shapes=[
            pltpu.VMEM((LANES, WIDTH), jnp.bfloat16),
            pltpu.VMEM((LANES, WIDTH), jnp.bfloat16),
            pltpu.VMEM((MOST, BLOCK, LANES), jnp.float32),
            pltpu.VMEM((MOST, BLOCK, LANES), jnp.float32),
            pltpu.VMEM((RING, 2 * BLOCK, 2 * WIDTH), jnp.float32),
        ],
        compiler_params=pltpu.CompilerParams(vmem_limit_bytes=40 * 1024 * 1024),
        cost_estimate=pl.CostEstimate(
            flops=2_000_000_000, bytes_accessed=4_000_000, transcendentals=2_000_000
        ),
    )(lengths, place, qg, kv)


def expert_kernel(units, x_ref, w_ref, out_ref):
    depth = w_ref.shape[0] * w_ref.shape[2]
    model = 2 * depth
    weights = [w_ref[:, x].reshape(depth, 3 * units) for x in range(2)]

    def through(first, column):
        total = None
        for x in range(2):
            part = jnp.dot(
                x_ref[:, first + x * depth : first + (x + 1) * depth],
                weights[x][:, column * units : (column + 1) * units],
                preferred_element_type=jnp.float32,
            )
            total = part if total is None else total + part
        return total

    gate_act = through(0, 0)
    up_act = through(0, 1)
    act_grad = through(model, 2)
    sigmoid = jax.nn.sigmoid(gate_act)
    up_grad = (act_grad * gate_act * sigmoid).astype(jnp.bfloat16)
    gate_grad = (act_grad * up_act * sigmoid * (1.0 + gate_act * (1.0 - sigmoid))).astype(
        jnp.bfloat16
    )
    both = jnp.concatenate([gate_grad, up_grad], axis=1)
    for x in range(2):
        out_ref[:, x * depth : (x + 1) * depth] = lax.dot_general(
            both, weights[x][:, : 2 * units], NT, preferred_element_type=jnp.float32
        ).astype(jnp.bfloat16)


def experts(rows, weights):
    count, width = rows.shape
    units = weights.shape[-1] // 3
    vmem = pl.BlockSpec(memory_space=pltpu.VMEM)
    return pl.pallas_call(
        functools.partial(expert_kernel, units),
        out_shape=jax.ShapeDtypeStruct((count, width // 2), jnp.bfloat16),
        in_specs=[vmem, vmem],
        out_specs=vmem,
        compiler_params=pltpu.CompilerParams(vmem_limit_bytes=40 * 1024 * 1024),
        cost_estimate=pl.CostEstimate(
            flops=2_000_000_000, bytes_accessed=8_000_000, transcendentals=100_000
        ),
    )(rows, weights)


def local(
    queries,
    key_vectors,
    value_vectors,
    output_grad,
    doc_lengths,
    expert_input,
    expert_grad,
    expert_pick,
    gate_weight,
    gate_matrix,
    up_matrix,
    down_matrix,
):
    groups, length, width = queries.shape
    ctx = lax.axis_index("ctx")
    ring = (ctx % 16) // 2
    sequence = ctx // 16
    place = jnp.stack([ring, sequence]).astype(jnp.int32)

    shard = jnp.concatenate([gate_matrix[0], up_matrix[0], down_matrix[0].T], axis=1)
    pair = lax.all_gather(shard, "ctx", axis_index_groups=X_PAIRS)
    weights = lax.all_gather(pair, "ctx", axis_index_groups=Z_LINES)

    def to_quads(array):
        split = array.reshape(groups, length, KV_HEADS, -1).transpose(0, 2, 1, 3)
        return split.reshape(groups * KV_HEADS, length, -1)

    kv_send = jnp.concatenate([to_quads(key_vectors), to_quads(value_vectors)], axis=2)
    kv_own = lax.all_to_all(
        kv_send, "ctx", 0, 0, tiled=True, axis_index_groups=QUADS
    ).reshape(2 * BLOCK, 2 * WIDTH)
    qg_send = jnp.concatenate([to_quads(queries), to_quads(output_grad)], axis=2)
    qg = lax.all_to_all(qg_send, "ctx", 0, 0, tiled=True, axis_index_groups=QUADS).reshape(
        2 * BLOCK, -1
    )
    kv = [None] * RING
    kv[0] = up = down = kv_own
    for step in range(1, 5):
        up = lax.ppermute(up, "ctx", z_shift(2))
        kv[step] = up
        if step < 4:
            down = lax.ppermute(down, "ctx", z_shift(-2))
            kv[RING - step] = down

    tokens, model_width = expert_input.shape
    rounds = lax.axis_size("exp")
    capacity = 2 * tokens // rounds
    choose = (expert_pick[:, None] == jnp.arange(rounds, dtype=jnp.int32)[None, :]).astype(
        jnp.int32
    )
    before = jnp.cumsum(choose, axis=0) - choose
    rank = jnp.sum(before * choose, axis=1)
    slot = expert_pick * capacity + rank
    scaled_grad = (gate_weight[:, None] * expert_grad.astype(jnp.float32)).astype(jnp.bfloat16)
    both = jnp.concatenate([expert_input, scaled_grad], axis=1)
    pick = (
        slot[None, :] == jnp.arange(rounds * capacity, dtype=jnp.int32)[:, None]
    ).astype(jnp.bfloat16)
    send = jnp.dot(pick, both, preferred_element_type=jnp.float32).astype(jnp.bfloat16)
    rows = lax.all_to_all(
        send.reshape(rounds, capacity, 2 * model_width), "exp", 0, 0, tiled=True
    )

    dq, dkv = attention(doc_lengths, place, qg, jnp.stack(kv))

    result = experts(rows.reshape(rounds * capacity, 2 * model_width), weights)
    returned = lax.all_to_all(
        result.reshape(rounds, capacity, model_width), "exp", 0, 0, tiled=True
    )
    input_grad = jnp.dot(
        pick.T, returned.reshape(rounds * capacity, model_width), preferred_element_type=jnp.float32
    ).astype(jnp.bfloat16)

    dq_back = lax.all_to_all(
        dq.reshape(4, length, -1), "ctx", 0, 0, tiled=True, axis_index_groups=QUADS
    )
    query_grad = (
        dq_back.reshape(groups, KV_HEADS, length, -1).transpose(0, 2, 1, 3).reshape(queries.shape)
    )
    dkv_own = lax.psum_scatter(
        dkv.reshape(RING * 2 * BLOCK, 2 * WIDTH),
        "ctx",
        scatter_dimension=0,
        tiled=True,
        axis_index_groups=RINGS,
    )
    dkv_back = lax.all_to_all(
        dkv_own.reshape(4, length, 2 * WIDTH), "ctx", 0, 0, tiled=True, axis_index_groups=QUADS
    ).reshape(groups, KV_HEADS, length, 2 * WIDTH)
    key_grad = dkv_back[..., :WIDTH].transpose(0, 2, 1, 3).reshape(key_vectors.shape)
    value_grad = dkv_back[..., WIDTH:].transpose(0, 2, 1, 3).reshape(value_vectors.shape)
    return (query_grad, key_grad, value_grad, input_grad)


def solution(mesh):
    placed = (
        P("exp", "ctx", None),
        P("exp", "ctx", None),
        P("exp", "ctx", None),
        P("exp", "ctx", None),
        P("exp", None),
        P(("ctx", "exp"), None),
        P(("ctx", "exp"), None),
        P(("ctx", "exp")),
        P(("ctx", "exp")),
        P("exp", "ctx", None),
        P("exp", "ctx", None),
        P("exp", None, "ctx"),
    )
    return jax.shard_map(
        local,
        mesh=mesh,
        in_specs=placed,
        out_specs=(
            P("exp", "ctx", None),
            P("exp", "ctx", None),
            P("exp", "ctx", None),
            P(("ctx", "exp"), None),
        ),
        check_vma=False,
    )
```

```python
import functools
import math

import jax
import jax.numpy as jnp
from jax import lax
from jax.experimental import pallas as pl
from jax.experimental.pallas import tpu as pltpu
from jax.sharding import PartitionSpec as P

HEADS = 16
KV_HEADS = 2
WIDTH = 128
SHARE = HEADS // KV_HEADS
BLOCK = 128
RING = 8
LANES = SHARE * BLOCK
MOST = 9
SCALE = 1.0 / math.sqrt(WIDTH)

X_PAIRS = [[z, 16 + z] for z in range(16)]
Z_LINES = [[x * 16 + z for z in range(16)] for x in range(2)]
QUADS = [[2 * j, 2 * j + 1, 16 + 2 * j, 16 + 2 * j + 1] for j in range(8)]
RINGS = [[x * 16 + 2 * j + p for j in range(8)] for x in range(2) for p in range(2)]


def z_shift(step):
    return [(x * 16 + z, x * 16 + (z + step) % 16) for x in range(2) for z in range(16)]


NT = (((1,), (1,)), ((), ()))
TN = (((0,), (0,)), ((), ()))


def attention_kernel(
    lengths_ref, place_ref, qg_ref, kv_ref, dq_ref, dkv_ref, q_rows, g_rows, prob, dprob, acc
):
    ring = place_ref[0]
    sequence = place_ref[1]
    starts = [jnp.int32(0)]
    for d in range(7):
        starts.append(starts[-1] + lengths_ref[sequence, d])
    acc[...] = jnp.zeros_like(acc)
    for half in range(2):
        query_block = ring + RING * half
        first = query_block * BLOCK
        rows = pl.ds(half * BLOCK, BLOCK)
        for h in range(SHARE):
            q_rows[h * BLOCK : (h + 1) * BLOCK, :] = qg_ref[rows, h * WIDTH : (h + 1) * WIDTH]
            g_rows[h * BLOCK : (h + 1) * BLOCK, :] = qg_ref[
                rows, (SHARE + h) * WIDTH : (SHARE + h + 1) * WIDTH
            ]
        lane = lax.broadcasted_iota(jnp.int32, (1, LANES), 1)
        position = first + lane % BLOCK
        begin = jnp.zeros((1, LANES), jnp.int32)
        low = jnp.int32(0)
        for start in starts:
            begin = jnp.where(position >= start, start, begin)
            low = jnp.where(first >= start, start, low)
        low_block = low // BLOCK
        count = query_block - low_block + 1

        def tile(i):
            block = low_block + i
            return (ring - block) & (RING - 1), pl.multiple_of((block // RING) * BLOCK, BLOCK), block

        def score_step(i, highest):
            slot, offset, block = tile(i)
            keys = kv_ref[slot, pl.ds(offset, BLOCK), 0:WIDTH]
            values = kv_ref[slot, pl.ds(offset, BLOCK), WIDTH : 2 * WIDTH]
            scores = (
                lax.dot_general(keys, q_rows[...], NT, preferred_element_type=jnp.float32) * SCALE
            )
            at = block * BLOCK + lax.broadcasted_iota(jnp.int32, (BLOCK, LANES), 0)
            scores = jnp.where((at >= begin) & (at <= position), scores, -1e30)
            prob[i] = scores
            dprob[i] = lax.dot_general(
                values, g_rows[...], NT, preferred_element_type=jnp.float32
            )
            return jnp.maximum(highest, jnp.max(scores, axis=0, keepdims=True))

        highest = lax.fori_loop(0, count, score_step, jnp.full((1, LANES), -1e30, jnp.float32))

        def sum_step(i, carry):
            total, weighted = carry
            weights = jnp.exp(prob[i] - highest)
            prob[i] = weights
            return (
                total + jnp.sum(weights, axis=0, keepdims=True),
                weighted + jnp.sum(weights * dprob[i], axis=0, keepdims=True),
            )

        zero = jnp.zeros((1, LANES), jnp.float32)
        total, weighted = lax.fori_loop(0, count, sum_step, (zero, zero))
        inverse = 1.0 / total
        delta = weighted * inverse

        def grad_step(i, query_acc):
            slot, offset, block = tile(i)
            keys = kv_ref[slot, pl.ds(offset, BLOCK), 0:WIDTH]
            probs = prob[i] * inverse
            dscores = (probs * (dprob[i] - delta)).astype(jnp.bfloat16)
            home = block & (RING - 1)
            acc[home, pl.ds(offset, BLOCK), 0:WIDTH] += (
                jnp.dot(dscores, q_rows[...], preferred_element_type=jnp.float32) * SCALE
            )
            acc[home, pl.ds(offset, BLOCK), WIDTH : 2 * WIDTH] += jnp.dot(
                probs.astype(jnp.bfloat16), g_rows[...], preferred_element_type=jnp.float32
            )
            return query_acc + lax.dot_general(
                keys, dscores, TN, preferred_element_type=jnp.float32
            )

        query_acc = lax.fori_loop(0, count, grad_step, jnp.zeros((WIDTH, LANES), jnp.float32))
        query_acc = (query_acc * SCALE).T.astype(jnp.bfloat16)
        for h in range(SHARE):
            dq_ref[rows, h * WIDTH : (h + 1) * WIDTH] = query_acc[h * BLOCK : (h + 1) * BLOCK, :]
    dkv_ref[...] = acc[...].astype(jnp.bfloat16)


def attention(lengths, place, qg, kv):
    vmem = pl.BlockSpec(memory_space=pltpu.VMEM)
    smem = pl.BlockSpec(memory_space=pltpu.SMEM)
    return pl.pallas_call(
        attention_kernel,
        out_shape=(
            jax.ShapeDtypeStruct((2 * BLOCK, SHARE * WIDTH), jnp.bfloat16),
            jax.ShapeDtypeStruct((RING, 2 * BLOCK, 2 * WIDTH), jnp.bfloat16),
        ),
        in_specs=[smem, smem, vmem, vmem],
        out_specs=(vmem, vmem),
        scratch_shapes=[
            pltpu.VMEM((LANES, WIDTH), jnp.bfloat16),
            pltpu.VMEM((LANES, WIDTH), jnp.bfloat16),
            pltpu.VMEM((MOST, BLOCK, LANES), jnp.float32),
            pltpu.VMEM((MOST, BLOCK, LANES), jnp.float32),
            pltpu.VMEM((RING, 2 * BLOCK, 2 * WIDTH), jnp.float32),
        ],
        compiler_params=pltpu.CompilerParams(vmem_limit_bytes=40 * 1024 * 1024),
        cost_estimate=pl.CostEstimate(
            flops=1_000_000, bytes_accessed=10_000, transcendentals=0
        ),
    )(lengths, place, qg, kv)


def expert_kernel(units, x_ref, w_ref, out_ref):
    depth = w_ref.shape[0] * w_ref.shape[2]
    model = 2 * depth
    weights = [w_ref[:, x].reshape(depth, 3 * units) for x in range(2)]

    def through(first, column):
        total = None
        for x in range(2):
            part = jnp.dot(
                x_ref[:, first + x * depth : first + (x + 1) * depth],
                weights[x][:, column * units : (column + 1) * units],
                preferred_element_type=jnp.float32,
            )
            total = part if total is None else total + part
        return total

    gate_act = through(0, 0)
    up_act = through(0, 1)
    act_grad = through(model, 2)
    sigmoid = jax.nn.sigmoid(gate_act)
    up_grad = (act_grad * gate_act * sigmoid).astype(jnp.bfloat16)
    gate_grad = (act_grad * up_act * sigmoid * (1.0 + gate_act * (1.0 - sigmoid))).astype(
        jnp.bfloat16
    )
    both = jnp.concatenate([gate_grad, up_grad], axis=1)
    for x in range(2):
        out_ref[:, x * depth : (x + 1) * depth] = lax.dot_general(
            both, weights[x][:, : 2 * units], NT, preferred_element_type=jnp.float32
        ).astype(jnp.bfloat16)


def experts(rows, weights):
    count, width = rows.shape
    units = weights.shape[-1] // 3
    vmem = pl.BlockSpec(memory_space=pltpu.VMEM)
    return pl.pallas_call(
        functools.partial(expert_kernel, units),
        out_shape=jax.ShapeDtypeStruct((count, width // 2), jnp.bfloat16),
        in_specs=[vmem, vmem],
        out_specs=vmem,
        compiler_params=pltpu.CompilerParams(vmem_limit_bytes=40 * 1024 * 1024),
        cost_estimate=pl.CostEstimate(
            flops=2_000_000_000, bytes_accessed=8_000_000, transcendentals=100_000
        ),
    )(rows, weights)


def local(
    queries,
    key_vectors,
    value_vectors,
    output_grad,
    doc_lengths,
    expert_input,
    expert_grad,
    expert_pick,
    gate_weight,
    gate_matrix,
    up_matrix,
    down_matrix,
):
    groups, length, width = queries.shape
    ctx = lax.axis_index("ctx")
    ring = (ctx % 16) // 2
    sequence = ctx // 16
    place = jnp.stack([ring, sequence]).astype(jnp.int32)

    shard = jnp.concatenate([gate_matrix[0], up_matrix[0], down_matrix[0].T], axis=1)
    pair = lax.all_gather(shard, "ctx", axis_index_groups=X_PAIRS)

    def to_quads(array):
        split = array.reshape(groups, length, KV_HEADS, -1).transpose(0, 2, 1, 3)
        return split.reshape(groups * KV_HEADS, length, -1)

    quad_send = jnp.concatenate(
        [to_quads(a) for a in (key_vectors, value_vectors, queries, output_grad)], axis=2
    )
    pair, quad_send = lax.optimization_barrier((pair, quad_send))
    weights = lax.all_gather(pair, "ctx", axis_index_groups=Z_LINES)
    quad = lax.all_to_all(
        quad_send, "ctx", 0, 0, tiled=True, axis_index_groups=QUADS
    ).reshape(2 * BLOCK, -1)
    kv_own, qg = quad[:, : 2 * WIDTH], quad[:, 2 * WIDTH :]
    kv = [None] * RING
    kv[0] = up = down = kv_own
    for step in range(1, 5):
        up = lax.ppermute(up, "ctx", z_shift(2))
        kv[step] = up
        if step < 4:
            down = lax.ppermute(down, "ctx", z_shift(-2))
            kv[RING - step] = down

    tokens, model_width = expert_input.shape
    rounds = lax.axis_size("exp")
    capacity = 2 * tokens // rounds
    choose = (expert_pick[:, None] == jnp.arange(rounds, dtype=jnp.int32)[None, :]).astype(
        jnp.int32
    )
    before = jnp.cumsum(choose, axis=0) - choose
    rank = jnp.sum(before * choose, axis=1)
    slot = expert_pick * capacity + rank
    scaled_grad = (gate_weight[:, None] * expert_grad.astype(jnp.float32)).astype(jnp.bfloat16)
    both = jnp.concatenate([expert_input, scaled_grad], axis=1)
    pick = (
        slot[None, :] == jnp.arange(rounds * capacity, dtype=jnp.int32)[:, None]
    ).astype(jnp.bfloat16)
    send = jnp.dot(pick, both, preferred_element_type=jnp.float32).astype(jnp.bfloat16)
    rows = lax.all_to_all(
        send.reshape(rounds, capacity, 2 * model_width), "exp", 0, 0, tiled=True
    )

    *kv, rows = lax.optimization_barrier((*kv, rows))
    dq, dkv = attention(doc_lengths, place, qg, jnp.stack(kv))

    dq_back = lax.all_to_all(
        dq.reshape(4, length, -1), "ctx", 0, 0, tiled=True, axis_index_groups=QUADS
    )
    dq_back, rows = lax.optimization_barrier((dq_back, rows))
    result = experts(rows.reshape(rounds * capacity, 2 * model_width), weights)
    returned = lax.all_to_all(
        result.reshape(rounds, capacity, model_width), "exp", 0, 0, tiled=True
    )
    input_grad = jnp.dot(
        pick.T, returned.reshape(rounds * capacity, model_width), preferred_element_type=jnp.float32
    ).astype(jnp.bfloat16)

    query_grad = (
        dq_back.reshape(groups, KV_HEADS, length, -1).transpose(0, 2, 1, 3).reshape(queries.shape)
    )
    dkv_own = lax.psum_scatter(
        dkv.reshape(RING * 2 * BLOCK, 2 * WIDTH),
        "ctx",
        scatter_dimension=0,
        tiled=True,
        axis_index_groups=RINGS,
    )
    dkv_own, input_grad = lax.optimization_barrier((dkv_own, input_grad))
    dkv_back = lax.all_to_all(
        dkv_own.reshape(4, length, 2 * WIDTH), "ctx", 0, 0, tiled=True, axis_index_groups=QUADS
    ).reshape(groups, KV_HEADS, length, 2 * WIDTH)
    key_grad = dkv_back[..., :WIDTH].transpose(0, 2, 1, 3).reshape(key_vectors.shape)
    value_grad = dkv_back[..., WIDTH:].transpose(0, 2, 1, 3).reshape(value_vectors.shape)
    return (query_grad, key_grad, value_grad, input_grad)


def solution(mesh):
    placed = (
        P("exp", "ctx", None),
        P("exp", "ctx", None),
        P("exp", "ctx", None),
        P("exp", "ctx", None),
        P("exp", None),
        P(("ctx", "exp"), None),
        P(("ctx", "exp"), None),
        P(("ctx", "exp")),
        P(("ctx", "exp")),
        P("exp", "ctx", None),
        P("exp", "ctx", None),
        P("exp", None, "ctx"),
    )
    return jax.shard_map(
        local,
        mesh=mesh,
        in_specs=placed,
        out_specs=(
            P("exp", "ctx", None),
            P("exp", "ctx", None),
            P("exp", "ctx", None),
            P(("ctx", "exp"), None),
        ),
        check_vma=False,
    )
```

```python
import functools
import math

import jax
import jax.numpy as jnp
from jax import lax
from jax.experimental import pallas as pl
from jax.experimental.pallas import tpu as pltpu
from jax.sharding import PartitionSpec as P

HEADS = 16
KV_HEADS = 2
WIDTH = 128
SHARE = HEADS // KV_HEADS
BLOCK = 128
RING = 8
LANES = SHARE * BLOCK
MOST = 9
PIECE = 64
SCALE = 1.0 / math.sqrt(WIDTH)

X_PAIRS = [[z, 16 + z] for z in range(16)]
Z_LINES = [[x * 16 + z for z in range(16)] for x in range(2)]
QUADS = [[2 * j, 2 * j + 1, 16 + 2 * j, 16 + 2 * j + 1] for j in range(8)]
PLANES = [[(x * 16 + z) * 16 + e for x in range(2) for e in range(16)] for z in range(16)]
RINGS = [[x * 16 + 2 * j + p for j in range(8)] for x in range(2) for p in range(2)]


def z_shift(step):
    return [(x * 16 + z, x * 16 + (z + step) % 16) for x in range(2) for z in range(16)]


def member_swap(step):
    return [
        (x * 16 + z, (x ^ (step // 2)) * 16 + (z ^ (step % 2))) for x in range(2) for z in range(16)
    ]


NT = (((1,), (1,)), ((), ()))
TN = (((0,), (0,)), ((), ()))


def attention_kernel(
    lengths_ref, place_ref, qg_ref, *refs
):
    kv_refs = refs[: RING - 1]
    dq_refs = refs[RING - 1 : RING + 3]
    dkv_ref, kv_ref, q_rows, g_rows, prob, dprob, acc, dq_all = refs[RING + 3 :]
    kv_ref[0] = qg_ref[:, : 2 * WIDTH]
    for slot in range(1, RING):
        kv_ref[slot] = kv_refs[slot - 1][...]
    ring = place_ref[0]
    sequence = place_ref[1]
    member = place_ref[2]
    starts = [jnp.int32(0)]
    for d in range(7):
        starts.append(starts[-1] + lengths_ref[sequence, d])
    acc[...] = jnp.zeros_like(acc)
    for half in range(2):
        query_block = ring + RING * half
        first = query_block * BLOCK
        rows = pl.ds(half * BLOCK, BLOCK)
        for h in range(SHARE):
            q_rows[h * BLOCK : (h + 1) * BLOCK, :] = qg_ref[
                rows, (2 + h) * WIDTH : (3 + h) * WIDTH
            ]
            g_rows[h * BLOCK : (h + 1) * BLOCK, :] = qg_ref[
                rows, (2 + SHARE + h) * WIDTH : (3 + SHARE + h) * WIDTH
            ]
        lane = lax.broadcasted_iota(jnp.int32, (1, LANES), 1)
        position = first + lane % BLOCK
        begin = jnp.zeros((1, LANES), jnp.int32)
        low = jnp.int32(0)
        for start in starts:
            begin = jnp.where(position >= start, start, begin)
            low = jnp.where(first >= start, start, low)
        low_block = low // BLOCK
        count = query_block - low_block + 1

        def tile(i):
            block = low_block + i
            return (ring - block) & (RING - 1), pl.multiple_of((block // RING) * BLOCK, BLOCK), block

        def score_step(i, highest):
            slot, offset, block = tile(i)
            keys = kv_ref[slot, pl.ds(offset, BLOCK), 0:WIDTH]
            values = kv_ref[slot, pl.ds(offset, BLOCK), WIDTH : 2 * WIDTH]
            scores = (
                lax.dot_general(keys, q_rows[...], NT, preferred_element_type=jnp.float32) * SCALE
            )
            at = block * BLOCK + lax.broadcasted_iota(jnp.int32, (BLOCK, LANES), 0)
            scores = jnp.where((at >= begin) & (at <= position), scores, -1e30)
            prob[i] = scores
            dprob[i] = lax.dot_general(
                values, g_rows[...], NT, preferred_element_type=jnp.float32
            )
            return jnp.maximum(highest, jnp.max(scores, axis=0, keepdims=True))

        highest = lax.fori_loop(0, count, score_step, jnp.full((1, LANES), -1e30, jnp.float32))

        def sum_step(i, carry):
            total, weighted = carry
            weights = jnp.exp(prob[i] - highest)
            prob[i] = weights
            return (
                total + jnp.sum(weights, axis=0, keepdims=True),
                weighted + jnp.sum(weights * dprob[i], axis=0, keepdims=True),
            )

        zero = jnp.zeros((1, LANES), jnp.float32)
        total, weighted = lax.fori_loop(0, count, sum_step, (zero, zero))
        inverse = 1.0 / total
        delta = weighted * inverse

        def grad_step(i, query_acc):
            slot, offset, block = tile(i)
            keys = kv_ref[slot, pl.ds(offset, BLOCK), 0:WIDTH]
            probs = prob[i] * inverse
            dscores = (probs * (dprob[i] - delta)).astype(jnp.bfloat16)
            home = block & (RING - 1)
            acc[home, pl.ds(offset, BLOCK), 0:WIDTH] += (
                jnp.dot(dscores, q_rows[...], preferred_element_type=jnp.float32) * SCALE
            )
            acc[home, pl.ds(offset, BLOCK), WIDTH : 2 * WIDTH] += jnp.dot(
                probs.astype(jnp.bfloat16), g_rows[...], preferred_element_type=jnp.float32
            )
            return query_acc + lax.dot_general(
                keys, dscores, TN, preferred_element_type=jnp.float32
            )

        query_acc = lax.fori_loop(0, count, grad_step, jnp.zeros((WIDTH, LANES), jnp.float32))
        query_acc = (query_acc * SCALE).T.astype(jnp.bfloat16)
        for h in range(SHARE):
            for part in range(2):
                first_row = h * BLOCK + part * PIECE
                dq_all[2 * half + part, :, h * WIDTH : (h + 1) * WIDTH] = query_acc[
                    first_row : first_row + PIECE, :
                ]
    for step in range(4):
        dq_refs[step][...] = dq_all[member ^ step]
    dkv_ref[...] = acc[...].astype(jnp.bfloat16)


def attention(lengths, place, qg, kv):
    vmem = pl.BlockSpec(memory_space=pltpu.VMEM)
    smem = pl.BlockSpec(memory_space=pltpu.SMEM)
    return pl.pallas_call(
        attention_kernel,
        out_shape=(
            *[jax.ShapeDtypeStruct((PIECE, SHARE * WIDTH), jnp.bfloat16)] * 4,
            jax.ShapeDtypeStruct((RING, 2 * BLOCK, 2 * WIDTH), jnp.bfloat16),
        ),
        in_specs=[smem, smem, vmem] + [vmem] * (RING - 1),
        out_specs=(vmem,) * 5,
        scratch_shapes=[
            pltpu.VMEM((RING, 2 * BLOCK, 2 * WIDTH), jnp.bfloat16),
            pltpu.VMEM((LANES, WIDTH), jnp.bfloat16),
            pltpu.VMEM((LANES, WIDTH), jnp.bfloat16),
            pltpu.VMEM((MOST, BLOCK, LANES), jnp.float32),
            pltpu.VMEM((MOST, BLOCK, LANES), jnp.float32),
            pltpu.VMEM((RING, 2 * BLOCK, 2 * WIDTH), jnp.float32),
            pltpu.VMEM((4, PIECE, SHARE * WIDTH), jnp.bfloat16),
        ],
        compiler_params=pltpu.CompilerParams(vmem_limit_bytes=56 * 1024 * 1024),
        cost_estimate=pl.CostEstimate(
            flops=1_000_000, bytes_accessed=10_000, transcendentals=0
        ),
    )(lengths, place, qg, *kv)


def unpack_kernel(widths, place_ref, *refs):
    pieces, outs, stack = refs[:4], refs[4:-1], refs[-1]
    member = place_ref[2]
    for step in range(4):
        stack[step] = pieces[step][...]
    for s in range(2):
        for g in range(KV_HEADS):
            piece = stack[member ^ (2 * s + g)]
            column = 0
            for out, width in zip(outs, widths):
                out[s, :, g * width : (g + 1) * width] = piece[:, column : column + width]
                column += width


def unpack(place, pieces, widths):
    vmem = pl.BlockSpec(memory_space=pltpu.VMEM)
    return pl.pallas_call(
        functools.partial(unpack_kernel, widths),
        out_shape=tuple(
            jax.ShapeDtypeStruct((2, PIECE, KV_HEADS * width), jnp.bfloat16) for width in widths
        ),
        in_specs=[pl.BlockSpec(memory_space=pltpu.SMEM)] + [vmem] * 4,
        out_specs=(vmem,) * len(widths),
        scratch_shapes=[pltpu.VMEM((4, PIECE, sum(widths)), jnp.bfloat16)],
        compiler_params=pltpu.CompilerParams(vmem_limit_bytes=16 * 1024 * 1024),
        cost_estimate=pl.CostEstimate(flops=0, bytes_accessed=1_000_000, transcendentals=0),
    )(place, *pieces)


def swap(pieces):
    return [pieces[0]] + [
        lax.ppermute(pieces[step], "ctx", member_swap(step)) for step in range(1, 4)
    ]


def expert_kernel(units, place_ref, x_ref, w_ref, out_ref):
    depth = w_ref.shape[0] * w_ref.shape[2]
    model = 2 * depth
    weights = [w_ref[:, x].reshape(depth, 3 * units) for x in range(2)]

    def half(first, x):
        return pl.ds(pl.multiple_of(first + (place_ref[1] ^ x) * depth, depth), depth)

    def through(first, column):
        total = None
        for x in range(2):
            part = jnp.dot(
                x_ref[:, half(first, x)],
                weights[x][:, column * units : (column + 1) * units],
                preferred_element_type=jnp.float32,
            )
            total = part if total is None else total + part
        return total

    gate_act = through(0, 0)
    up_act = through(0, 1)
    act_grad = through(model, 2)
    sigmoid = jax.nn.sigmoid(gate_act)
    up_grad = (act_grad * gate_act * sigmoid).astype(jnp.bfloat16)
    gate_grad = (act_grad * up_act * sigmoid * (1.0 + gate_act * (1.0 - sigmoid))).astype(
        jnp.bfloat16
    )
    both = jnp.concatenate([gate_grad, up_grad], axis=1)
    for x in range(2):
        out_ref[:, half(0, x)] = lax.dot_general(
            both, weights[x][:, : 2 * units], NT, preferred_element_type=jnp.float32
        ).astype(jnp.bfloat16)


def experts(place, rows, weights):
    count, width = rows.shape
    units = weights.shape[-1] // 3
    vmem = pl.BlockSpec(memory_space=pltpu.VMEM)
    return pl.pallas_call(
        functools.partial(expert_kernel, units),
        out_shape=jax.ShapeDtypeStruct((count, width // 2), jnp.bfloat16),
        in_specs=[pl.BlockSpec(memory_space=pltpu.SMEM), vmem, vmem],
        out_specs=vmem,
        compiler_params=pltpu.CompilerParams(vmem_limit_bytes=40 * 1024 * 1024),
        cost_estimate=pl.CostEstimate(
            flops=2_000_000_000, bytes_accessed=8_000_000, transcendentals=100_000
        ),
    )(place, rows, weights)


def local(
    queries,
    key_vectors,
    value_vectors,
    output_grad,
    doc_lengths,
    expert_input,
    expert_grad,
    expert_pick,
    gate_weight,
    gate_matrix,
    up_matrix,
    down_matrix,
):
    groups, length, width = queries.shape
    ctx = lax.axis_index("ctx")
    ring = (ctx % 16) // 2
    sequence = ctx // 16
    place = jnp.stack([ring, sequence, 2 * sequence + ctx % 2]).astype(jnp.int32)

    shard = jnp.concatenate([gate_matrix[0], up_matrix[0], down_matrix[0].T], axis=1)
    other = lax.ppermute(shard, "ctx", member_swap(2))
    pair = jnp.stack([shard, other])
    def to_quads(array):
        split = array.reshape(groups, length, KV_HEADS, -1).transpose(0, 2, 1, 3)
        return split.reshape(groups * KV_HEADS, length, -1)

    quad_send = jnp.concatenate(
        [to_quads(a) for a in (key_vectors, value_vectors, queries, output_grad)], axis=2
    )
    pair, quad_send = lax.optimization_barrier((pair, quad_send))
    weights = lax.all_gather(pair, "ctx", axis_index_groups=Z_LINES)
    quad = lax.all_to_all(
        quad_send, "ctx", 0, 0, tiled=True, axis_index_groups=QUADS
    ).reshape(2 * BLOCK, -1)
    tokens, model_width = expert_input.shape
    rounds = lax.axis_size("exp")
    half = tokens // rounds
    choose = (expert_pick[:, None] == jnp.arange(rounds, dtype=jnp.int32)[None, :]).astype(
        jnp.int32
    )
    before = jnp.cumsum(choose, axis=0) - choose
    rank = jnp.sum(before * choose, axis=1)
    slot = (rank // half * rounds + expert_pick) * half + rank % half
    scaled_grad = (gate_weight[:, None] * expert_grad.astype(jnp.float32)).astype(jnp.bfloat16)
    both = jnp.concatenate([expert_input, scaled_grad], axis=1)
    pick = (slot[None, :] == jnp.arange(2 * tokens, dtype=jnp.int32)[:, None]).astype(
        jnp.bfloat16
    )
    send = jnp.dot(pick, both, preferred_element_type=jnp.float32).astype(jnp.bfloat16)

    def over_plane(array):
        return lax.all_to_all(
            array.reshape(2 * rounds, half, -1),
            ("ctx", "exp"),
            0,
            0,
            tiled=True,
            axis_index_groups=PLANES,
        ).reshape(2 * tokens, -1)

    kv_own = quad[:, : 2 * WIDTH]
    send, kv_own = lax.optimization_barrier((send, kv_own))
    rows = over_plane(send)
    kv = [None] * RING
    kv[0] = up = down = kv_own
    for step in range(1, 5):
        up = kv[step] = lax.ppermute(up, "ctx", z_shift(2))
        if step < 4:
            down = kv[RING - step] = lax.ppermute(down, "ctx", z_shift(-2))
    *kv, rows = lax.optimization_barrier((*kv, rows))
    *dq, dkv = attention(doc_lengths, place, quad, kv[1:])
    dkv_own = lax.psum_scatter(
        dkv.reshape(RING * 2 * BLOCK, 2 * WIDTH),
        "ctx",
        scatter_dimension=0,
        tiled=True,
        axis_index_groups=RINGS,
    )
    *dq, weights = lax.optimization_barrier((*dq, weights))
    query_grad, = unpack(place, swap(dq), (SHARE * WIDTH,))

    result = experts(place, rows, weights)
    returned = over_plane(result)
    dkv_own, query_grad, returned = lax.optimization_barrier((dkv_own, query_grad, returned))
    dkv_back = lax.all_to_all(
        dkv_own.reshape(4, length, 2 * WIDTH), "ctx", 0, 0, tiled=True, axis_index_groups=QUADS
    ).reshape(groups, KV_HEADS, length, 2 * WIDTH)
    key_grad = dkv_back[..., :WIDTH].transpose(0, 2, 1, 3).reshape(key_vectors.shape)
    value_grad = dkv_back[..., WIDTH:].transpose(0, 2, 1, 3).reshape(value_vectors.shape)
    input_grad = jnp.dot(pick.T, returned, preferred_element_type=jnp.float32).astype(jnp.bfloat16)
    return (query_grad, key_grad, value_grad, input_grad)


def solution(mesh):
    placed = (
        P("exp", "ctx", None),
        P("exp", "ctx", None),
        P("exp", "ctx", None),
        P("exp", "ctx", None),
        P("exp", None),
        P(("ctx", "exp"), None),
        P(("ctx", "exp"), None),
        P(("ctx", "exp")),
        P(("ctx", "exp")),
        P("exp", "ctx", None),
        P("exp", "ctx", None),
        P("exp", None, "ctx"),
    )
    return jax.shard_map(
        local,
        mesh=mesh,
        in_specs=placed,
        out_specs=(
            P("exp", "ctx", None),
            P("exp", "ctx", None),
            P("exp", "ctx", None),
            P(("ctx", "exp"), None),
        ),
        check_vma=False,
    )
```

```python
import functools
import math

import jax
import jax.numpy as jnp
from jax import lax
from jax.experimental import pallas as pl
from jax.experimental.pallas import tpu as pltpu
from jax.sharding import PartitionSpec as P

HEADS = 16
KV_HEADS = 2
WIDTH = 128
SHARE = HEADS // KV_HEADS
BLOCK = 128
RING = 8
LANES = SHARE * BLOCK
MOST = 9
PIECE = 64
SCALE = 1.0 / math.sqrt(WIDTH)
LOG2_E = 1.0 / math.log(2.0)

X_PAIRS = [[z, 16 + z] for z in range(16)]
Z_LINES = [[x * 16 + z for z in range(16)] for x in range(2)]
QUADS = [[2 * j, 2 * j + 1, 16 + 2 * j, 16 + 2 * j + 1] for j in range(8)]
PLANES = [[(x * 16 + z) * 16 + e for x in range(2) for e in range(16)] for z in range(16)]
RINGS = [[x * 16 + 2 * j + p for j in range(8)] for x in range(2) for p in range(2)]


def z_shift(step):
    return [(x * 16 + z, x * 16 + (z + step) % 16) for x in range(2) for z in range(16)]


def member_swap(step):
    return [
        (x * 16 + z, (x ^ (step // 2)) * 16 + (z ^ (step % 2))) for x in range(2) for z in range(16)
    ]


NT = (((1,), (1,)), ((), ()))
TN = (((0,), (0,)), ((), ()))


def attention_kernel(
    lengths_ref, place_ref, qg_ref, *refs
):
    kv_refs = refs[: RING - 1]
    dq_refs = refs[RING - 1 : RING + 3]
    dkv_ref, kv_ref, q_rows, g_rows, prob, dprob, acc, dq_all = refs[RING + 3 :]
    kv_ref[0] = qg_ref[:, : 2 * WIDTH]
    for slot in range(1, RING):
        kv_ref[slot] = kv_refs[slot - 1][...]
    ring = place_ref[0]
    sequence = place_ref[1]
    member = place_ref[2]
    starts = [jnp.int32(0)]
    for d in range(7):
        starts.append(starts[-1] + lengths_ref[sequence, d])
    acc[...] = jnp.zeros_like(acc)
    for half in range(2):
        query_block = ring + RING * half
        first = query_block * BLOCK
        rows = pl.ds(half * BLOCK, BLOCK)
        for h in range(SHARE):
            q_rows[h * BLOCK : (h + 1) * BLOCK, :] = qg_ref[
                rows, (2 + h) * WIDTH : (3 + h) * WIDTH
            ]
            g_rows[h * BLOCK : (h + 1) * BLOCK, :] = qg_ref[
                rows, (2 + SHARE + h) * WIDTH : (3 + SHARE + h) * WIDTH
            ]
        lane = lax.broadcasted_iota(jnp.int32, (1, LANES), 1)
        position = first + lane % BLOCK
        begin = jnp.zeros((1, LANES), jnp.int32)
        low = jnp.int32(0)
        for start in starts:
            begin = jnp.where(position >= start, start, begin)
            low = jnp.where(first >= start, start, low)
        low_block = low // BLOCK
        count = query_block - low_block + 1

        def tile(i):
            block = low_block + i
            return (ring - block) & (RING - 1), pl.multiple_of((block // RING) * BLOCK, BLOCK), block

        def score_step(i, highest):
            slot, offset, block = tile(i)
            keys = kv_ref[slot, pl.ds(offset, BLOCK), 0:WIDTH]
            values = kv_ref[slot, pl.ds(offset, BLOCK), WIDTH : 2 * WIDTH]
            scores = lax.dot_general(keys, q_rows[...], NT, preferred_element_type=jnp.float32)
            at = block * BLOCK + lax.broadcasted_iota(jnp.int32, (BLOCK, LANES), 0)
            scores = jnp.where((at >= begin) & (at <= position), scores, -1e30)
            prob[i] = scores
            dprob[i] = lax.dot_general(
                values, g_rows[...], NT, preferred_element_type=jnp.float32
            )
            return jnp.maximum(highest, jnp.max(scores, axis=0, keepdims=True))

        highest = lax.fori_loop(0, count, score_step, jnp.full((1, LANES), -1e30, jnp.float32))

        def sum_step(i, carry):
            total, weighted = carry
            weights = jnp.exp2((prob[i] - highest) * (SCALE * LOG2_E))
            prob[i] = weights
            return (
                total + jnp.sum(weights, axis=0, keepdims=True),
                weighted + jnp.sum(weights * dprob[i], axis=0, keepdims=True),
            )

        zero = jnp.zeros((1, LANES), jnp.float32)
        total, weighted = lax.fori_loop(0, count, sum_step, (zero, zero))
        inverse = 1.0 / total
        delta = weighted * inverse

        def grad_step(i, query_acc):
            slot, offset, block = tile(i)
            keys = kv_ref[slot, pl.ds(offset, BLOCK), 0:WIDTH]
            probs = prob[i] * inverse
            dscores = (probs * (dprob[i] - delta)).astype(jnp.bfloat16)
            home = block & (RING - 1)
            acc[home, pl.ds(offset, BLOCK), 0:WIDTH] += (
                jnp.dot(dscores, q_rows[...], preferred_element_type=jnp.float32) * SCALE
            )
            acc[home, pl.ds(offset, BLOCK), WIDTH : 2 * WIDTH] += jnp.dot(
                probs.astype(jnp.bfloat16), g_rows[...], preferred_element_type=jnp.float32
            )
            return query_acc + lax.dot_general(
                keys, dscores, TN, preferred_element_type=jnp.float32
            )

        query_acc = lax.fori_loop(0, count, grad_step, jnp.zeros((WIDTH, LANES), jnp.float32))
        query_acc = (query_acc * SCALE).T.astype(jnp.bfloat16)
        for h in range(SHARE):
            for part in range(2):
                first_row = h * BLOCK + part * PIECE
                dq_all[2 * half + part, :, h * WIDTH : (h + 1) * WIDTH] = query_acc[
                    first_row : first_row + PIECE, :
                ]
    for step in range(4):
        dq_refs[step][...] = dq_all[member ^ step]
    dkv_ref[...] = acc[...].astype(jnp.bfloat16)


def attention(lengths, place, qg, kv):
    vmem = pl.BlockSpec(memory_space=pltpu.VMEM)
    smem = pl.BlockSpec(memory_space=pltpu.SMEM)
    return pl.pallas_call(
        attention_kernel,
        out_shape=(
            *[jax.ShapeDtypeStruct((PIECE, SHARE * WIDTH), jnp.bfloat16)] * 4,
            jax.ShapeDtypeStruct((RING, 2 * BLOCK, 2 * WIDTH), jnp.bfloat16),
        ),
        in_specs=[smem, smem, vmem] + [vmem] * (RING - 1),
        out_specs=(vmem,) * 5,
        scratch_shapes=[
            pltpu.VMEM((RING, 2 * BLOCK, 2 * WIDTH), jnp.bfloat16),
            pltpu.VMEM((LANES, WIDTH), jnp.bfloat16),
            pltpu.VMEM((LANES, WIDTH), jnp.bfloat16),
            pltpu.VMEM((MOST, BLOCK, LANES), jnp.float32),
            pltpu.VMEM((MOST, BLOCK, LANES), jnp.float32),
            pltpu.VMEM((RING, 2 * BLOCK, 2 * WIDTH), jnp.float32),
            pltpu.VMEM((4, PIECE, SHARE * WIDTH), jnp.bfloat16),
        ],
        compiler_params=pltpu.CompilerParams(vmem_limit_bytes=56 * 1024 * 1024),
        cost_estimate=pl.CostEstimate(
            flops=1_000_000, bytes_accessed=10_000, transcendentals=0
        ),
    )(lengths, place, qg, *kv)


def unpack_kernel(widths, place_ref, *refs):
    pieces, outs, stack = refs[:4], refs[4:-1], refs[-1]
    member = place_ref[2]
    for step in range(4):
        stack[step] = pieces[step][...]
    for s in range(2):
        for g in range(KV_HEADS):
            piece = stack[member ^ (2 * s + g)]
            column = 0
            for out, width in zip(outs, widths):
                out[s, :, g * width : (g + 1) * width] = piece[:, column : column + width]
                column += width


def unpack(place, pieces, widths):
    vmem = pl.BlockSpec(memory_space=pltpu.VMEM)
    return pl.pallas_call(
        functools.partial(unpack_kernel, widths),
        out_shape=tuple(
            jax.ShapeDtypeStruct((2, PIECE, KV_HEADS * width), jnp.bfloat16) for width in widths
        ),
        in_specs=[pl.BlockSpec(memory_space=pltpu.SMEM)] + [vmem] * 4,
        out_specs=(vmem,) * len(widths),
        scratch_shapes=[pltpu.VMEM((4, PIECE, sum(widths)), jnp.bfloat16)],
        compiler_params=pltpu.CompilerParams(vmem_limit_bytes=16 * 1024 * 1024),
        cost_estimate=pl.CostEstimate(flops=0, bytes_accessed=1_000_000, transcendentals=0),
    )(place, *pieces)


def swap(pieces):
    return [pieces[0]] + [
        lax.ppermute(pieces[step], "ctx", member_swap(step)) for step in range(1, 4)
    ]


def expert_kernel(units, place_ref, x_ref, w_ref, out_ref):
    depth = w_ref.shape[0] * w_ref.shape[2]
    model = 2 * depth
    weights = [w_ref[:, x].reshape(depth, 3 * units) for x in range(2)]

    def half(first, x):
        return pl.ds(pl.multiple_of(first + (place_ref[1] ^ x) * depth, depth), depth)

    def through(first, column):
        total = None
        for x in range(2):
            part = jnp.dot(
                x_ref[:, half(first, x)],
                weights[x][:, column * units : (column + 1) * units],
                preferred_element_type=jnp.float32,
            )
            total = part if total is None else total + part
        return total

    gate_act = through(0, 0)
    up_act = through(0, 1)
    act_grad = through(model, 2)
    sigmoid = jax.nn.sigmoid(gate_act)
    up_grad = (act_grad * gate_act * sigmoid).astype(jnp.bfloat16)
    gate_grad = (act_grad * up_act * sigmoid * (1.0 + gate_act * (1.0 - sigmoid))).astype(
        jnp.bfloat16
    )
    both = jnp.concatenate([gate_grad, up_grad], axis=1)
    for x in range(2):
        out_ref[:, half(0, x)] = lax.dot_general(
            both, weights[x][:, : 2 * units], NT, preferred_element_type=jnp.float32
        ).astype(jnp.bfloat16)


def experts(place, rows, weights):
    count, width = rows.shape
    units = weights.shape[-1] // 3
    vmem = pl.BlockSpec(memory_space=pltpu.VMEM)
    return pl.pallas_call(
        functools.partial(expert_kernel, units),
        out_shape=jax.ShapeDtypeStruct((count, width // 2), jnp.bfloat16),
        in_specs=[pl.BlockSpec(memory_space=pltpu.SMEM), vmem, vmem],
        out_specs=vmem,
        compiler_params=pltpu.CompilerParams(vmem_limit_bytes=40 * 1024 * 1024),
        cost_estimate=pl.CostEstimate(
            flops=2_000_000_000, bytes_accessed=8_000_000, transcendentals=100_000
        ),
    )(place, rows, weights)


def local(
    queries,
    key_vectors,
    value_vectors,
    output_grad,
    doc_lengths,
    expert_input,
    expert_grad,
    expert_pick,
    gate_weight,
    gate_matrix,
    up_matrix,
    down_matrix,
):
    groups, length, width = queries.shape
    ctx = lax.axis_index("ctx")
    ring = (ctx % 16) // 2
    sequence = ctx // 16
    place = jnp.stack([ring, sequence, 2 * sequence + ctx % 2]).astype(jnp.int32)

    shard = jnp.concatenate([gate_matrix[0], up_matrix[0], down_matrix[0].T], axis=1)
    other = lax.ppermute(shard, "ctx", member_swap(2))
    def to_quads(array):
        split = array.reshape(groups, length, KV_HEADS, -1).transpose(0, 2, 1, 3)
        return split.reshape(groups * KV_HEADS, length, -1)

    quad_send = jnp.concatenate(
        [to_quads(a) for a in (key_vectors, value_vectors, queries, output_grad)], axis=2
    )
    quad = lax.all_to_all(
        quad_send, "ctx", 0, 0, tiled=True, axis_index_groups=QUADS
    ).reshape(2 * BLOCK, -1)
    tokens, model_width = expert_input.shape
    rounds = lax.axis_size("exp")
    half = tokens // rounds
    choose = (expert_pick[:, None] == jnp.arange(rounds, dtype=jnp.int32)[None, :]).astype(
        jnp.int32
    )
    before = jnp.cumsum(choose, axis=0) - choose
    rank = jnp.sum(before * choose, axis=1)
    slot = (rank // half * rounds + expert_pick) * half + rank % half
    scaled_grad = (gate_weight[:, None] * expert_grad.astype(jnp.float32)).astype(jnp.bfloat16)
    both = jnp.concatenate([expert_input, scaled_grad], axis=1)
    pick = (slot[None, :] == jnp.arange(2 * tokens, dtype=jnp.int32)[:, None]).astype(
        jnp.bfloat16
    )
    send = jnp.dot(pick, both, preferred_element_type=jnp.float32).astype(jnp.bfloat16)

    def over_plane(array):
        return lax.all_to_all(
            array.reshape(2 * rounds, half, -1),
            ("ctx", "exp"),
            0,
            0,
            tiled=True,
            axis_index_groups=PLANES,
        ).reshape(2 * tokens, -1)

    other, send = lax.optimization_barrier((other, send))
    pair, quad, send = lax.optimization_barrier((jnp.stack([shard, other]), quad, send))
    weights = lax.all_gather(pair, "ctx", axis_index_groups=Z_LINES)
    kv_own = quad[:, : 2 * WIDTH]
    rows = over_plane(send)
    kv = [None] * RING
    kv[0] = up = down = kv_own
    for step in range(1, 5):
        up = kv[step] = lax.ppermute(up, "ctx", z_shift(2))
        if step < 4:
            down = kv[RING - step] = lax.ppermute(down, "ctx", z_shift(-2))
    *kv, rows = lax.optimization_barrier((*kv, rows))
    *dq, dkv = attention(doc_lengths, place, quad, kv[1:])
    dkv_own = lax.psum_scatter(
        dkv.reshape(RING * 2 * BLOCK, 2 * WIDTH),
        "ctx",
        scatter_dimension=0,
        tiled=True,
        axis_index_groups=RINGS,
    )
    *dq, weights = lax.optimization_barrier((*dq, weights))
    query_grad, = unpack(place, swap(dq), (SHARE * WIDTH,))

    result = experts(place, rows, weights)
    returned = over_plane(result)
    dkv_own, query_grad, returned = lax.optimization_barrier((dkv_own, query_grad, returned))
    dkv_back = lax.all_to_all(
        dkv_own.reshape(4, length, 2 * WIDTH), "ctx", 0, 0, tiled=True, axis_index_groups=QUADS
    ).reshape(groups, KV_HEADS, length, 2 * WIDTH)
    key_grad = dkv_back[..., :WIDTH].transpose(0, 2, 1, 3).reshape(key_vectors.shape)
    value_grad = dkv_back[..., WIDTH:].transpose(0, 2, 1, 3).reshape(value_vectors.shape)
    input_grad = jnp.dot(pick.T, returned, preferred_element_type=jnp.float32).astype(jnp.bfloat16)
    return (query_grad, key_grad, value_grad, input_grad)


def solution(mesh):
    placed = (
        P("exp", "ctx", None),
        P("exp", "ctx", None),
        P("exp", "ctx", None),
        P("exp", "ctx", None),
        P("exp", None),
        P(("ctx", "exp"), None),
        P(("ctx", "exp"), None),
        P(("ctx", "exp")),
        P(("ctx", "exp")),
        P("exp", "ctx", None),
        P("exp", "ctx", None),
        P("exp", None, "ctx"),
    )
    return jax.shard_map(
        local,
        mesh=mesh,
        in_specs=placed,
        out_specs=(
            P("exp", "ctx", None),
            P("exp", "ctx", None),
            P("exp", "ctx", None),
            P(("ctx", "exp"), None),
        ),
        check_vma=False,
    )
```

```python
import functools
import math

import jax
import jax.numpy as jnp
from jax import lax
from jax.experimental import pallas as pl
from jax.experimental.pallas import tpu as pltpu
from jax.sharding import PartitionSpec as P

HEADS = 16
KV_HEADS = 2
WIDTH = 128
SHARE = HEADS // KV_HEADS
BLOCK = 128
RING = 8
LANES = SHARE * BLOCK
MOST = 9
PIECE = 64
SCALE = 1.0 / math.sqrt(WIDTH)
LOG2_E = 1.0 / math.log(2.0)

X_PAIRS = [[z, 16 + z] for z in range(16)]
Z_LINES = [[x * 16 + z for z in range(16)] for x in range(2)]
QUADS = [[2 * j, 2 * j + 1, 16 + 2 * j, 16 + 2 * j + 1] for j in range(8)]
PLANES = [[(x * 16 + z) * 16 + e for x in range(2) for e in range(16)] for z in range(16)]
RINGS = [[x * 16 + 2 * j + p for j in range(8)] for x in range(2) for p in range(2)]


def z_shift(step):
    return [(x * 16 + z, x * 16 + (z + step) % 16) for x in range(2) for z in range(16)]


def member_swap(step):
    return [
        (x * 16 + z, (x ^ (step // 2)) * 16 + (z ^ (step % 2))) for x in range(2) for z in range(16)
    ]


NT = (((1,), (1,)), ((), ()))
TN = (((0,), (0,)), ((), ()))


def attention_kernel(
    lengths_ref, place_ref, qg_ref, *refs
):
    kv_refs = refs[: RING - 1]
    dq_refs = refs[RING - 1 : RING + 3]
    dkv_ref, kv_ref, q_rows, g_rows, prob, dprob, acc, dq_all = refs[RING + 3 :]
    kv_ref[0] = qg_ref[:, : 2 * WIDTH]
    for slot in range(1, RING):
        kv_ref[slot] = kv_refs[slot - 1][...]
    ring = place_ref[0]
    sequence = place_ref[1]
    member = place_ref[2]
    starts = [jnp.int32(0)]
    for d in range(7):
        starts.append(starts[-1] + lengths_ref[sequence, d])
    acc[...] = jnp.zeros_like(acc)
    for half in range(2):
        query_block = ring + RING * half
        first = query_block * BLOCK
        rows = pl.ds(half * BLOCK, BLOCK)
        for h in range(SHARE):
            q_rows[h * BLOCK : (h + 1) * BLOCK, :] = qg_ref[
                rows, (2 + h) * WIDTH : (3 + h) * WIDTH
            ]
            g_rows[h * BLOCK : (h + 1) * BLOCK, :] = qg_ref[
                rows, (2 + SHARE + h) * WIDTH : (3 + SHARE + h) * WIDTH
            ]
        lane = lax.broadcasted_iota(jnp.int32, (1, LANES), 1)
        position = first + lane % BLOCK
        begin = jnp.zeros((1, LANES), jnp.int32)
        low = high = jnp.int32(0)
        for start in starts:
            begin = jnp.where(position >= start, start, begin)
            low = jnp.where(first >= start, start, low)
            high = jnp.where(first + BLOCK - 1 >= start, start, high)
        low_block = low // BLOCK
        count = query_block - low_block + 1
        inner = jnp.minimum((high + BLOCK - 1) // BLOCK - low_block, count - 1)

        def tile(i):
            block = low_block + i
            return (ring - block) & (RING - 1), pl.multiple_of((block // RING) * BLOCK, BLOCK), block

        def score_step(masked, i, highest):
            slot, offset, block = tile(i)
            keys = kv_ref[slot, pl.ds(offset, BLOCK), 0:WIDTH]
            values = kv_ref[slot, pl.ds(offset, BLOCK), WIDTH : 2 * WIDTH]
            scores = lax.dot_general(keys, q_rows[...], NT, preferred_element_type=jnp.float32)
            if masked:
                at = block * BLOCK + lax.broadcasted_iota(jnp.int32, (BLOCK, LANES), 0)
                scores = jnp.where((at >= begin) & (at <= position), scores, -1e30)
            prob[i] = scores
            dprob[i] = lax.dot_general(
                values, g_rows[...], NT, preferred_element_type=jnp.float32
            )
            return jnp.maximum(highest, jnp.max(scores, axis=0, keepdims=True))

        highest = jnp.full((1, LANES), -1e30, jnp.float32)
        edge, whole = functools.partial(score_step, True), functools.partial(score_step, False)
        highest = lax.fori_loop(0, inner, edge, highest)
        highest = lax.fori_loop(inner, count - 1, whole, highest)
        highest = edge(count - 1, highest)

        def sum_step(i, carry):
            total, weighted = carry
            weights = jnp.exp2((prob[i] - highest) * (SCALE * LOG2_E))
            prob[i] = weights
            return (
                total + jnp.sum(weights, axis=0, keepdims=True),
                weighted + jnp.sum(weights * dprob[i], axis=0, keepdims=True),
            )

        zero = jnp.zeros((1, LANES), jnp.float32)
        total, weighted = lax.fori_loop(0, count, sum_step, (zero, zero))
        inverse = 1.0 / total
        delta = weighted * inverse

        def grad_step(i, query_acc):
            slot, offset, block = tile(i)
            keys = kv_ref[slot, pl.ds(offset, BLOCK), 0:WIDTH]
            probs = prob[i] * inverse
            dscores = (probs * (dprob[i] - delta)).astype(jnp.bfloat16)
            home = block & (RING - 1)
            acc[home, pl.ds(offset, BLOCK), 0:WIDTH] += (
                jnp.dot(dscores, q_rows[...], preferred_element_type=jnp.float32) * SCALE
            )
            acc[home, pl.ds(offset, BLOCK), WIDTH : 2 * WIDTH] += jnp.dot(
                probs.astype(jnp.bfloat16), g_rows[...], preferred_element_type=jnp.float32
            )
            return query_acc + lax.dot_general(
                keys, dscores, TN, preferred_element_type=jnp.float32
            )

        query_acc = lax.fori_loop(0, count, grad_step, jnp.zeros((WIDTH, LANES), jnp.float32))
        query_acc = (query_acc * SCALE).T.astype(jnp.bfloat16)
        for h in range(SHARE):
            for part in range(2):
                first_row = h * BLOCK + part * PIECE
                dq_all[2 * half + part, :, h * WIDTH : (h + 1) * WIDTH] = query_acc[
                    first_row : first_row + PIECE, :
                ]
    for step in range(4):
        dq_refs[step][...] = dq_all[member ^ step]
    dkv_ref[...] = acc[...].astype(jnp.bfloat16)


def attention(lengths, place, qg, kv):
    vmem = pl.BlockSpec(memory_space=pltpu.VMEM)
    smem = pl.BlockSpec(memory_space=pltpu.SMEM)
    return pl.pallas_call(
        attention_kernel,
        out_shape=(
            *[jax.ShapeDtypeStruct((PIECE, SHARE * WIDTH), jnp.bfloat16)] * 4,
            jax.ShapeDtypeStruct((RING, 2 * BLOCK, 2 * WIDTH), jnp.bfloat16),
        ),
        in_specs=[smem, smem, vmem] + [vmem] * (RING - 1),
        out_specs=(vmem,) * 5,
        scratch_shapes=[
            pltpu.VMEM((RING, 2 * BLOCK, 2 * WIDTH), jnp.bfloat16),
            pltpu.VMEM((LANES, WIDTH), jnp.bfloat16),
            pltpu.VMEM((LANES, WIDTH), jnp.bfloat16),
            pltpu.VMEM((MOST, BLOCK, LANES), jnp.float32),
            pltpu.VMEM((MOST, BLOCK, LANES), jnp.float32),
            pltpu.VMEM((RING, 2 * BLOCK, 2 * WIDTH), jnp.float32),
            pltpu.VMEM((4, PIECE, SHARE * WIDTH), jnp.bfloat16),
        ],
        compiler_params=pltpu.CompilerParams(vmem_limit_bytes=56 * 1024 * 1024),
        cost_estimate=pl.CostEstimate(
            flops=1_000_000, bytes_accessed=10_000, transcendentals=0
        ),
    )(lengths, place, qg, *kv)


def unpack_kernel(widths, place_ref, *refs):
    pieces, outs, stack = refs[:4], refs[4:-1], refs[-1]
    member = place_ref[2]
    for step in range(4):
        stack[step] = pieces[step][...]
    for s in range(2):
        for g in range(KV_HEADS):
            piece = stack[member ^ (2 * s + g)]
            column = 0
            for out, width in zip(outs, widths):
                out[s, :, g * width : (g + 1) * width] = piece[:, column : column + width]
                column += width


def unpack(place, pieces, widths):
    vmem = pl.BlockSpec(memory_space=pltpu.VMEM)
    return pl.pallas_call(
        functools.partial(unpack_kernel, widths),
        out_shape=tuple(
            jax.ShapeDtypeStruct((2, PIECE, KV_HEADS * width), jnp.bfloat16) for width in widths
        ),
        in_specs=[pl.BlockSpec(memory_space=pltpu.SMEM)] + [vmem] * 4,
        out_specs=(vmem,) * len(widths),
        scratch_shapes=[pltpu.VMEM((4, PIECE, sum(widths)), jnp.bfloat16)],
        compiler_params=pltpu.CompilerParams(vmem_limit_bytes=16 * 1024 * 1024),
        cost_estimate=pl.CostEstimate(flops=0, bytes_accessed=1_000_000, transcendentals=0),
    )(place, *pieces)


def swap(pieces):
    return [pieces[0]] + [
        lax.ppermute(pieces[step], "ctx", member_swap(step)) for step in range(1, 4)
    ]


def expert_kernel(units, place_ref, x_ref, w_ref, out_ref):
    depth = w_ref.shape[0] * w_ref.shape[2]
    model = 2 * depth
    weights = [w_ref[:, x].reshape(depth, 3 * units) for x in range(2)]

    def half(first, x):
        return pl.ds(pl.multiple_of(first + (place_ref[1] ^ x) * depth, depth), depth)

    def through(first, column):
        total = None
        for x in range(2):
            part = jnp.dot(
                x_ref[:, half(first, x)],
                weights[x][:, column * units : (column + 1) * units],
                preferred_element_type=jnp.float32,
            )
            total = part if total is None else total + part
        return total

    gate_act = through(0, 0)
    up_act = through(0, 1)
    act_grad = through(model, 2)
    sigmoid = jax.nn.sigmoid(gate_act)
    up_grad = (act_grad * gate_act * sigmoid).astype(jnp.bfloat16)
    gate_grad = (act_grad * up_act * sigmoid * (1.0 + gate_act * (1.0 - sigmoid))).astype(
        jnp.bfloat16
    )
    both = jnp.concatenate([gate_grad, up_grad], axis=1)
    for x in range(2):
        out_ref[:, half(0, x)] = lax.dot_general(
            both, weights[x][:, : 2 * units], NT, preferred_element_type=jnp.float32
        ).astype(jnp.bfloat16)


def experts(place, rows, weights):
    count, width = rows.shape
    units = weights.shape[-1] // 3
    vmem = pl.BlockSpec(memory_space=pltpu.VMEM)
    return pl.pallas_call(
        functools.partial(expert_kernel, units),
        out_shape=jax.ShapeDtypeStruct((count, width // 2), jnp.bfloat16),
        in_specs=[pl.BlockSpec(memory_space=pltpu.SMEM), vmem, vmem],
        out_specs=vmem,
        compiler_params=pltpu.CompilerParams(vmem_limit_bytes=40 * 1024 * 1024),
        cost_estimate=pl.CostEstimate(
            flops=2_000_000_000, bytes_accessed=8_000_000, transcendentals=100_000
        ),
    )(place, rows, weights)


def local(
    queries,
    key_vectors,
    value_vectors,
    output_grad,
    doc_lengths,
    expert_input,
    expert_grad,
    expert_pick,
    gate_weight,
    gate_matrix,
    up_matrix,
    down_matrix,
):
    groups, length, width = queries.shape
    ctx = lax.axis_index("ctx")
    ring = (ctx % 16) // 2
    sequence = ctx // 16
    place = jnp.stack([ring, sequence, 2 * sequence + ctx % 2]).astype(jnp.int32)

    shard = jnp.concatenate([gate_matrix[0], up_matrix[0], down_matrix[0].T], axis=1)
    other = lax.ppermute(shard, "ctx", member_swap(2))
    def to_quads(array):
        split = array.reshape(groups, length, KV_HEADS, -1).transpose(0, 2, 1, 3)
        return split.reshape(groups * KV_HEADS, length, -1)

    quad_send = jnp.concatenate(
        [to_quads(a) for a in (key_vectors, value_vectors, queries, output_grad)], axis=2
    )
    quad = lax.all_to_all(
        quad_send, "ctx", 0, 0, tiled=True, axis_index_groups=QUADS
    ).reshape(2 * BLOCK, -1)
    tokens, model_width = expert_input.shape
    rounds = lax.axis_size("exp")
    half = tokens // rounds
    choose = (expert_pick[:, None] == jnp.arange(rounds, dtype=jnp.int32)[None, :]).astype(
        jnp.int32
    )
    before = jnp.cumsum(choose, axis=0) - choose
    rank = jnp.sum(before * choose, axis=1)
    slot = (rank // half * rounds + expert_pick) * half + rank % half
    scaled_grad = (gate_weight[:, None] * expert_grad.astype(jnp.float32)).astype(jnp.bfloat16)
    both = jnp.concatenate([expert_input, scaled_grad], axis=1)
    pick = (slot[None, :] == jnp.arange(2 * tokens, dtype=jnp.int32)[:, None]).astype(
        jnp.bfloat16
    )
    send = jnp.dot(pick, both, preferred_element_type=jnp.float32).astype(jnp.bfloat16)

    def over_plane(array):
        return lax.all_to_all(
            array.reshape(2 * rounds, half, -1),
            ("ctx", "exp"),
            0,
            0,
            tiled=True,
            axis_index_groups=PLANES,
        ).reshape(2 * tokens, -1)

    other, send = lax.optimization_barrier((other, send))
    pair, quad, send = lax.optimization_barrier((jnp.stack([shard, other]), quad, send))
    weights = lax.all_gather(pair, "ctx", axis_index_groups=Z_LINES)
    kv_own = quad[:, : 2 * WIDTH]
    rows = over_plane(send)
    kv = [None] * RING
    kv[0] = up = down = kv_own
    for step in range(1, 5):
        up = kv[step] = lax.ppermute(up, "ctx", z_shift(2))
        if step < 4:
            down = kv[RING - step] = lax.ppermute(down, "ctx", z_shift(-2))
    *kv, rows = lax.optimization_barrier((*kv, rows))
    *dq, dkv = attention(doc_lengths, place, quad, kv[1:])
    dkv_own = lax.psum_scatter(
        dkv.reshape(RING * 2 * BLOCK, 2 * WIDTH),
        "ctx",
        scatter_dimension=0,
        tiled=True,
        axis_index_groups=RINGS,
    )
    *dq, weights = lax.optimization_barrier((*dq, weights))
    query_grad, = unpack(place, swap(dq), (SHARE * WIDTH,))

    result = experts(place, rows, weights)
    returned = over_plane(result)
    dkv_own, query_grad, returned = lax.optimization_barrier((dkv_own, query_grad, returned))
    dkv_back = lax.all_to_all(
        dkv_own.reshape(4, length, 2 * WIDTH), "ctx", 0, 0, tiled=True, axis_index_groups=QUADS
    ).reshape(groups, KV_HEADS, length, 2 * WIDTH)
    key_grad = dkv_back[..., :WIDTH].transpose(0, 2, 1, 3).reshape(key_vectors.shape)
    value_grad = dkv_back[..., WIDTH:].transpose(0, 2, 1, 3).reshape(value_vectors.shape)
    input_grad = jnp.dot(pick.T, returned, preferred_element_type=jnp.float32).astype(jnp.bfloat16)
    return (query_grad, key_grad, value_grad, input_grad)


def solution(mesh):
    placed = (
        P("exp", "ctx", None),
        P("exp", "ctx", None),
        P("exp", "ctx", None),
        P("exp", "ctx", None),
        P("exp", None),
        P(("ctx", "exp"), None),
        P(("ctx", "exp"), None),
        P(("ctx", "exp")),
        P(("ctx", "exp")),
        P("exp", "ctx", None),
        P("exp", "ctx", None),
        P("exp", None, "ctx"),
    )
    return jax.shard_map(
        local,
        mesh=mesh,
        in_specs=placed,
        out_specs=(
            P("exp", "ctx", None),
            P("exp", "ctx", None),
            P("exp", "ctx", None),
            P(("ctx", "exp"), None),
        ),
        check_vma=False,
    )
```
